512 devices in a mesh: lat: 64 (over x, y, z_lo), lev: 8 (over z_hi, core).
Axes of the slice: x: 4, y: 8, z: 8 (z_hi: 4, z_lo: 2; z = z_hi * 2 + z_lo), core: 2. Of those that a mesh axis runs over, the one named last changes fastest.
Arguments:
- winds: float32 [2, 16, 256, 1152], P(None, 'lev', 'lat'), may hold values from -5 to 5
- fields: float32 [5, 16, 256, 1152], P(None, 'lev', 'lat'), may hold values from -6 to 6
- thickness: float32 [16, 256, 1152], P('lev', 'lat'), may hold values from 0.5 to 2
- filter_mask: int32 [256], P('lat'), may hold values from 0 to 1
- cutoff: int32 [256], P('lat'), may hold values from 1 to 576
Outputs:
- winds_out: float32 [2, 16, 256, 1152], P(None, 'lev', 'lat')
- fields_out: float32 [5, 16, 256, 1152], P(None, 'lev', 'lat')
- column_mass: float32 [256, 1152], P('lat', 'lev')
The draws below stay inside these ranges and needn't reach their ends.
All inputs are finite; a program needn't handle non-finite values.
Results may differ from the reference program's by a relative error of at most 0.0003.
Values sent between devices are 32-bit elements; how exact they have to be, the bound alone decides.
No kernel may reach another device: no remote copies, remote signals or barrier semaphores. Data moves between devices by JAX's collectives and lax.ppermute only.
A program may use at most 64 MiB of HBM per device.

```python
import jax
import jax.numpy as jnp
from jax import lax

NLON = 1152
NSUB = 2
NLAT = 256
LEV = 16


def pole_distance():
    row_ids = jnp.arange(NLAT, dtype=jnp.int32)
    return jnp.minimum(row_ids, NLAT - 1 - row_ids)


def draw_filter_mask(key, part):
    key = jax.random.fold_in(key, 11)
    distance = pole_distance()
    coin = jax.random.randint(key, (NLAT,), 0, 2)
    core = (distance < NLAT // 8).astype(jnp.int32)
    fringe = jnp.logical_and(distance >= NLAT // 8, distance < 3 * NLAT // 16).astype(jnp.int32)
    return (core + fringe * coin).astype(jnp.int32)


def draw_cutoff(key, part):
    key = jax.random.fold_in(key, 23)
    distance = pole_distance()
    jitter = jax.random.randint(key, (NLAT,), 0, 3)
    base = 1 + distance * (NLON // 2 - 2) // (NLAT // 4) + jitter * (distance > 0).astype(jnp.int32)
    return jnp.minimum(base, NLON // 2).astype(jnp.int32)


def block_scale(stream_key, extent, pieces, smallest, largest):
    def one(dim, parts):
        heights = jax.random.uniform(jax.random.fold_in(jax.random.fold_in(stream_key, 6), dim), (parts,), jnp.float32, smallest / len(pieces), largest / len(pieces))
        return jnp.repeat(jnp.exp(heights), extent[dim] // parts).reshape((-1,) + (1,) * (len(extent) - dim - 1))

    loudness = one(*pieces[0])
    for cut in pieces[1:]:
        loudness = loudness * one(*cut)
    return loudness


def centred(own_key, extent, scale, most, pieces=(), kind=jnp.bfloat16):
    entries = scale * jax.random.normal(own_key, extent, jnp.float32)
    if pieces:
        entries = entries * block_scale(own_key, extent, pieces, -0.22, 0.18)
    return jnp.clip(entries, -most, most).astype(kind)


def setup_inputs(seed: int = 0) -> dict:
    key_list = jax.random.split(jax.random.key(seed), 6)
    winds = centred(key_list[0], (2, LEV, NLAT, NLON), 1.0, 5.0, ((1, 8), (2, 64)), jnp.float32)
    fields = centred(key_list[1], (5, LEV, NLAT, NLON), 1.0, 6.0, ((1, 8), (2, 64)), jnp.float32)
    thickness = jnp.clip(0.5 + 1.5 * jax.random.uniform(key_list[2], (LEV, NLAT, NLON), jnp.float32) ** block_scale(key_list[2], (LEV, NLAT, NLON), ((0, 8), (1, 64)), -0.2, 0.2), 0.5, 2.0)
    filter_mask = draw_filter_mask(jax.random.fold_in(key_list[5], 71), 0)
    cutoff = draw_cutoff(jax.random.fold_in(key_list[5], 71), 0)
    return {"winds": winds, "fields": fields, "thickness": thickness, "filter_mask": filter_mask, "cutoff": cutoff}


CX_COEF = 0.08
CY_COEF = 0.08


def fromm_flux(courant, center, before, after, beyond):
    return courant * jnp.where(courant >= 0.0,
                               center + (1.0 - courant) * 0.25 * (after - before),
                               after - (1.0 + courant) * 0.25 * (beyond - center))


def advect(padded, courant_x, courant_y):
    row_count = padded.shape[-2]
    face_x = 0.5 * (courant_x + jnp.roll(courant_x, -1, axis=-1))
    flux_x = fromm_flux(face_x, padded, jnp.roll(padded, 1, axis=-1), jnp.roll(padded, -1, axis=-1), jnp.roll(padded, -2, axis=-1))
    diverge_x = flux_x - jnp.roll(flux_x, 1, axis=-1)
    face_y = 0.5 * (courant_y[..., 1:row_count - 2, :] + courant_y[..., 2:row_count - 1, :])
    flux_y = fromm_flux(face_y, padded[..., 1:row_count - 2, :], padded[..., 0:row_count - 3, :],
                        padded[..., 2:row_count - 1, :], padded[..., 3:row_count, :])
    diverge_y = flux_y[..., 1:, :] - flux_y[..., :-1, :]
    return padded[..., 2:row_count - 2, :] - diverge_x[..., 2:row_count - 2, :] - diverge_y


def damping(mask, cutoff, length):
    wavenum = jnp.arange(1, length // 2 + 1).astype(jnp.float32)
    ratio = cutoff.astype(jnp.float32)[:, None] / wavenum[None, :]
    return jnp.maximum(0.0, 1.0 - ratio * ratio) * mask.astype(jnp.float32)[:, None]


def polar_filter(wind_pair, mask, cutoff):
    length = wind_pair.shape[-1]
    damp = damping(mask, cutoff, length)
    damp = jnp.concatenate([jnp.zeros((damp.shape[0], 1), jnp.float32), damp], axis=1)
    spectra = jnp.fft.rfft(wind_pair, axis=-1)
    removed = jnp.fft.irfft(spectra * damp, n=length, axis=-1)
    return wind_pair - removed.astype(wind_pair.dtype)


def remap_columns(prognostic):
    thick = prognostic[2]
    upper_edge = jnp.cumsum(thick, axis=0)
    lower_edge = jnp.concatenate([jnp.zeros_like(upper_edge[:1]), upper_edge[:-1]], axis=0)
    column_total = upper_edge[-1]
    levels = thick.shape[0]
    carried = jnp.concatenate([prognostic[:2], prognostic[3:]], axis=0)
    scale = float(levels) / column_total

    def one_layer(target):
        lower = column_total * (target.astype(jnp.float32) / levels)
        upper = column_total * ((target + 1).astype(jnp.float32) / levels)
        intersection = jnp.maximum(0.0, jnp.minimum(upper_edge, upper) - jnp.maximum(lower_edge, lower))
        return jnp.einsum("fkrl,krl->frl", carried, intersection, precision=lax.Precision.HIGHEST) * scale

    layers = lax.map(one_layer, jnp.arange(levels, dtype=jnp.int32))
    return jnp.transpose(layers, (1, 0, 2, 3)), column_total


def reference(winds, fields, thickness, filter_mask, cutoff):
    prognostic = jnp.concatenate([winds, thickness[None], fields], axis=0)
    for substep in range(NSUB):
        padded = jnp.pad(prognostic, ((0, 0), (0, 0), (2, 2), (0, 0)))
        courant_x = CX_COEF * padded[0]
        courant_y = CY_COEF * padded[1]
        prognostic = lax.map(lambda single: advect(single, courant_x, courant_y), padded)
        prognostic = jnp.concatenate([polar_filter(prognostic[:2], filter_mask, cutoff), prognostic[2:]], axis=0)
    layers, column_total = remap_columns(prognostic)
    return layers[:2], layers[2:], column_total
```

```python
import math

import jax
import jax.numpy as jnp
import numpy as np
from jax import lax
from jax.experimental import pallas as pl
from jax.experimental.pallas import tpu as pltpu
from jax.sharding import PartitionSpec as P

NSUB = 2
COEF = 0.08
LANES = 128
RADIX = 9
LON = RADIX * LANES
HALF = RADIX // 2 + 1
ROWS = 4
TILES = 16
EXTRA = 16


def make_tables():
    n2 = np.arange(LANES)
    k1 = np.arange(HALF)
    theta = 2.0 * math.pi * k1[:, None] * n2[None, :] / LON
    k = k1[:, None] + RADIX * n2[None, :]
    k = np.minimum(k, LON - k)
    inverse = np.where(k > 0, 1.0 / np.maximum(k, 1) ** 2, 0.0)
    scale = np.where(k > 0, np.where(k1[:, None] == 0, 1.0, 2.0) / LON, 0.0)
    table = np.zeros((4, 8, LANES), np.float32)
    table[0, :HALF] = np.cos(theta)
    table[1, :HALF] = np.sin(theta)
    table[2, :HALF] = inverse
    table[3, :HALF] = scale
    angle = 2.0 * math.pi * (n2[:, None] * n2[None, :] % LANES) / LANES
    cosine, sine = np.cos(angle), np.sin(angle)
    dense = np.block([[cosine, -sine], [sine, cosine]]).astype(np.float32)
    high = dense.astype(jnp.bfloat16)
    low = (dense - high.astype(np.float32)).astype(jnp.bfloat16)
    return table, high, low


def split_dot(left, high, low):
    left_high = left.astype(jnp.bfloat16)
    left_low = (left - left_high.astype(jnp.float32)).astype(jnp.bfloat16)
    dot = lambda a, b: jnp.dot(a, b, preferred_element_type=jnp.float32)
    return dot(left_high, high) + (dot(left_low, high) + dot(left_high, low))


def polar_filter(rows, wind_ref, square_ref, keep_ref, table_ref, high_ref, low_ref):
    blocks = [wind_ref[:rows, LANES * j : LANES * (j + 1)] for j in range(RADIX)]
    plus = [blocks[j] + blocks[RADIX - j] for j in range(1, HALF)]
    minus = [blocks[j] - blocks[RADIX - j] for j in range(1, HALF)]
    cosine = lambda a: math.cos(2.0 * math.pi * (a % RADIX) / RADIX)
    sine = lambda a: math.sin(2.0 * math.pi * (a % RADIX) / RADIX)
    real, imag = [blocks[0] + ((plus[0] + plus[1]) + (plus[2] + plus[3]))], [jnp.zeros_like(blocks[0])]
    for k in range(1, HALF):
        re = blocks[0]
        im = None
        for j in range(1, HALF):
            re = re + cosine(j * k) * plus[j - 1]
            term = sine(j * k) * minus[j - 1]
            im = -term if im is None else im - term
        turn_c = table_ref[0, k : k + 1, :]
        turn_s = table_ref[1, k : k + 1, :]
        real.append(re * turn_c + im * turn_s)
        imag.append(im * turn_c - re * turn_s)
    stacked = jnp.concatenate(
        [jnp.concatenate(real, axis=0), jnp.concatenate(imag, axis=0)], axis=1
    )
    high, low = high_ref[...], low_ref[...]
    spectra = split_dot(stacked, high, low)
    square, keep = square_ref[:rows], keep_ref[:rows]
    damped_re, damped_im = [], []
    for k in range(HALF):
        damp = jnp.maximum(0.0, 1.0 - square * table_ref[2, k : k + 1, :])
        damp = damp * (keep * table_ref[3, k : k + 1, :])
        damped_re.append(spectra[rows * k : rows * (k + 1), :LANES] * damp)
        damped_im.append(spectra[rows * k : rows * (k + 1), LANES:] * -damp)
    damped = jnp.concatenate(
        [jnp.concatenate(damped_re, axis=0), jnp.concatenate(damped_im, axis=0)], axis=1
    )
    back = split_dot(damped, high, low)
    first = back[:rows, :LANES]
    real, imag = [], []
    for k in range(1, HALF):
        re = back[rows * k : rows * (k + 1), :LANES]
        im = back[rows * k : rows * (k + 1), LANES:]
        turn_c = table_ref[0, k : k + 1, :]
        turn_s = table_ref[1, k : k + 1, :]
        real.append(re * turn_c + im * turn_s)
        imag.append(re * turn_s - im * turn_c)
    out = [blocks[0] - (first + ((real[0] + real[1]) + (real[2] + real[3])))] + [None] * (RADIX - 1)
    for n in range(1, HALF):
        even = first
        odd = None
        for k in range(1, HALF):
            even = even + cosine(n * k) * real[k - 1]
            term = sine(n * k) * imag[k - 1]
            odd = term if odd is None else odd + term
        out[n] = blocks[n] - (even - odd)
        out[RADIX - n] = blocks[RADIX - n] - (even + odd)
    return out


def face_weights(courant):
    up = jnp.maximum(courant, 0.0)
    down = jnp.minimum(courant, 0.0)
    a = 0.25 * up * (1.0 - up)
    d = 0.25 * down * (1.0 + down)
    return a, up + d, down + a, d


def advect_rows(count, row_of, store, u_ref, v_ref, weight_ref):
    for r in range(count):
        u_ref[r : r + 1, :] = row_of(r)[0:1]
    for r in range(-1, count + 1):
        v_ref[r + 1 : r + 2, :] = row_of(r)[1:2]
    u = COEF * u_ref[:count]
    a, b, c, d = face_weights(0.5 * (u + pltpu.roll(u, LON - 1, 1)))
    back = lambda x: pltpu.roll(x, 1, 1)
    weight_ref[0, :count] = -back(a)
    weight_ref[1, :count] = a + back(b)
    weight_ref[3, :count] = -(c + back(d))
    weight_ref[4, :count] = d
    center = 1.0 - (b - back(c))
    a, b, c, d = face_weights((0.5 * COEF) * (v_ref[: count + 1] + v_ref[1 : count + 2]))
    weight_ref[5, :count] = -a[:count]
    weight_ref[6, :count] = a[1:] + b[:count]
    weight_ref[2, :count] = center - (b[1:] - c[:count])
    weight_ref[7, :count] = -(c[1:] + d[:count])
    weight_ref[8, :count] = d[1:]
    for r in range(count):
        weight = lambda n: weight_ref[n, r : r + 1, :]
        q = row_of(r)
        new = weight(2) * q
        for n, step in ((0, 2), (1, 1), (3, LON - 1), (4, LON - 2)):
            new = new + weight(n) * pltpu.roll(q, step, 1)
        for n, step in ((5, -2), (6, -1), (7, 1), (8, 2)):
            new = new + weight(n) * row_of(r + step)
        store(r, new)


def pack_kernel(
    mask_hbm, cutoff_hbm, winds_hbm, fields_hbm, thick_hbm, mine_ref, other_ref,
    mask_ref, cutoff_ref, winds_ref, fields_ref, thick_ref, sems,
):
    copies = [
        pltpu.make_async_copy(source, target, sems.at[i])
        for i, (source, target) in enumerate(
            (
                (mask_hbm, mask_ref), (cutoff_hbm, cutoff_ref),
                (winds_hbm, winds_ref), (fields_hbm, fields_ref), (thick_hbm, thick_ref),
            )
        )
    ]
    for copy in copies:
        copy.start()
    half = lax.axis_index("half")
    copies[0].wait()
    copies[1].wait()
    for ref in (mine_ref, other_ref):
        for r in range(ROWS):
            cut = cutoff_ref[r].astype(jnp.float32)
            ref[ROWS * RADIX, r : r + 1, :] = jnp.full((1, LANES), cut * cut, jnp.float32)
            ref[ROWS * RADIX, ROWS + r : ROWS + r + 1, :] = jnp.full(
                (1, LANES), mask_ref[r].astype(jnp.float32), jnp.float32
            )
    for copy in copies[2:]:
        copy.wait()
    for ref, level in ((mine_ref, half), (other_ref, 1 - half)):
        for f in range(8):
            for r in range(ROWS):
                if f < 2:
                    row = winds_ref[f, level, r : r + 1, :]
                elif f == 2:
                    row = thick_ref[level, r : r + 1, :]
                else:
                    row = fields_ref[f - 3, level, r : r + 1, :]
                for b in range(RADIX):
                    ref[RADIX * r + b, f : f + 1, :] = row[:, LANES * b : LANES * (b + 1)]


def unpack_rows(parts, start_ref, meta_ref):
    for ref, group in parts:
        for r in range(ROWS):
            for b in range(RADIX):
                start_ref[ROWS * group + r, :, LANES * b : LANES * (b + 1)] = ref[RADIX * r + b]
        meta_ref[group] = ref[ROWS * RADIX]


def substep(count, row_of, meta_of, limit, target_ref, tables, work):
    wind_ref, square_ref, keep_ref, u_ref, v_ref, weight_ref = work

    def store(r, new):
        new = limit(r, new)
        target_ref[r] = new
        wind_ref[2 * r : 2 * r + 2, :] = new[0:2]

    advect_rows(count, row_of, store, u_ref, v_ref, weight_ref)
    for r in range(count):
        for ref, value in zip((square_ref, keep_ref), meta_of(r)):
            ref[2 * r : 2 * r + 2, :] = jnp.broadcast_to(value, (2, LANES))
    blocks = polar_filter(2 * count, wind_ref, square_ref, keep_ref, *tables)
    for j in range(RADIX):
        for r in range(count):
            target_ref[r, 0:2, LANES * j : LANES * (j + 1)] = blocks[j][2 * r : 2 * r + 2]


def meta_rows(meta_ref, first):
    def meta_of(r):
        group, at = (first + r) // ROWS, (first + r) % ROWS
        return meta_ref[group, at : at + 1, :], meta_ref[group, ROWS + at : ROWS + at + 1, :]

    return meta_of


def outside(r, count, edge):
    half = lax.axis_index("half")
    pair = lax.axis_index("pair")
    if r < 2:
        return jnp.logical_and(half == edge, pair == 0)
    if r >= count - 2:
        return jnp.logical_and(half == 1 - edge, pair == lax.axis_size("pair") - 1)
    return None


def limiter(count, edge):
    def limit(r, new):
        beyond = outside(r, count, edge)
        return new if beyond is None else jnp.where(beyond, 0.0, new)

    return limit


def pack_band(final_ref, put, turned_ref):
    group = lax.broadcasted_iota(jnp.int32, (8, LANES), 1) // EXTRA
    extras = [None] * 8
    for r in range(ROWS):
        blocks = [final_ref[r, :, LANES * b : LANES * (b + 1)] for b in range(RADIX)]
        for owner in range(8):
            value = jnp.where(
                group < 8 - owner, turn(blocks[owner], -owner), turn(blocks[owner + 1], -owner)
            )
            turned_ref[pl.ds(32 * owner + r, 8, stride=4), :] = value
            extra = turn(blocks[owner + 1], r - owner)
            extras[owner] = extra if r == 0 else jnp.where(group == r, extra, extras[owner])
    for owner in range(8):
        put(owner, 8, jnp.where(group[:4] < 4, extras[owner][:4], swap(extras[owner])[4:]))
        for f in range(8):
            put(owner, f, turned_ref[32 * owner + 4 * f : 32 * owner + 4 * f + 4, :])


def early_kernel(
    mine_ref, partner_ref, near_ref, table_ref, high_ref, low_ref, early_ref, band_ref,
    start_ref, meta_ref, final_ref, turned_ref, *work,
):
    half = lax.axis_index("half")
    tables = (table_ref, high_ref, low_ref)
    unpack_rows(
        ((mine_ref, 2 * half), (partner_ref, 1), (near_ref, 2 - 2 * half)), start_ref, meta_ref
    )
    substep(
        2 * ROWS, lambda r: start_ref[r + 2], meta_rows(meta_ref, 2), limiter(2 * ROWS, 1),
        early_ref, tables, work,
    )
    substep(
        ROWS, lambda r: early_ref[r + 2], meta_rows(meta_ref, ROWS), lambda r, new: new, final_ref,
        tables, work,
    )

    def put(owner, tile, value):
        band_ref[owner, tile] = value

    pack_band(final_ref, put, turned_ref)


def late_kernel(
    mine_ref, far_ref, early_ref, band_ref, table_ref, high_ref, low_ref, send_ref,
    start_ref, meta_ref, rest_ref, first_ref, final_ref, turned_ref, *work,
):
    half = lax.axis_index("half")
    tables = (table_ref, high_ref, low_ref)
    for owner in range(8):
        send_ref[8 * (1 - half) + owner] = band_ref[owner]
    for r in range(ROWS):
        first_ref[ROWS * (1 - half) + r] = early_ref[ROWS * half + r]
    unpack_rows(((mine_ref, 1 - half), (far_ref, half)), start_ref, meta_ref)
    substep(
        ROWS, lambda r: start_ref[r + 2], meta_rows(meta_ref, 2), limiter(ROWS, 0), rest_ref, tables,
        work,
    )
    for r in range(ROWS):
        first_ref[ROWS * half + r] = rest_ref[r]
    meta_ref[0] = mine_ref[ROWS * RADIX]
    substep(
        ROWS, lambda r: first_ref[r + 2], meta_rows(meta_ref, 0), lambda r, new: new, final_ref,
        tables, work,
    )

    def put(owner, tile, value):
        send_ref[8 * half + owner, tile] = value

    pack_band(final_ref, put, turned_ref)


def turn(x, steps):
    return pltpu.roll(x, EXTRA * (steps % 8), 1) if steps % 8 else x


def swap(x):
    return turn(x, 4)


def tile_of(f, level):
    return 7 * level + (f if f < 2 else f - 1)


def remap_kernel(got_ref, send_ref, mass_ref, edge_ref):
    levels = 16
    pairs = ((0, 1), (3, 4), (5, 6), (7, 7))
    both = lambda source, a, b: jnp.concatenate([got_ref[source, a], got_ref[source, b]], axis=0)
    inside = lambda lower, upper, low, high: jnp.maximum(
        0.0, jnp.minimum(upper, high) - jnp.maximum(lower, low)
    )
    add = lambda total, term: term if total is None else total + term

    edges = [jnp.zeros((8, LANES), jnp.float32)]
    for k in range(levels):
        edges.append(edges[-1] + both(8 * (k % 2) + k // 2, 2, 2))
    mass = edges[-1]
    scale = float(levels) / mass
    for i in range(levels + 1):
        edge_ref[i] = edges[i]
    chunk = 8
    for first in range(0, levels, chunk):
        bounds = [mass * (m / levels) for m in range(first, first + chunk + 1)]
        totals = [[None] * len(pairs) for _ in range(chunk)]
        for k in range(levels):
            lower, upper = edge_ref[k], edge_ref[k + 1]
            values = [both(8 * (k % 2) + k // 2, a, b) for a, b in pairs]
            for m in range(chunk):
                overlap = inside(lower, upper, bounds[m], bounds[m + 1])
                for p, value in enumerate(values):
                    totals[m][p] = add(totals[m][p], value * overlap)
        for m in range(chunk):
            target, level = (first + m) // 2, (first + m) % 2
            for p, (a, b) in enumerate(pairs):
                total = totals[m][p] * scale
                send_ref[target, tile_of(a, level)] = total[:4]
                if b != a:
                    send_ref[target, tile_of(b, level)] = total[4:]
    mass_ref[:, :LANES] = mass[:4]

    left = lax.broadcasted_iota(jnp.int32, (8, LANES), 1) < LANES // 2
    base = jnp.zeros((8, LANES), jnp.float32)
    steps = []
    for k in range(levels // 2):
        even, odd = got_ref[k, 8], got_ref[8 + k, 8]
        value = jnp.concatenate(
            [jnp.where(left[:4], even, swap(odd)), jnp.where(left[:4], swap(even), odd)], axis=0
        )
        thick = jnp.broadcast_to(value[2:3], (8, LANES))
        other = swap(thick)
        lower = base + jnp.where(left, 0.0, other)
        upper = lower + thick
        base = jnp.where(left, upper + other, upper)
        steps.append((value, lower, upper))
    scale = float(levels) / base
    bounds = [base * (m / levels) for m in range(levels + 1)]
    totals = [None] * levels
    for value, lower, upper in steps:
        for m in range(levels):
            totals[m] = add(totals[m], value * inside(lower, upper, bounds[m], bounds[m + 1]))
    totals = [(total + swap(total)) * scale for total in totals]
    for m in range(0, levels, 2):
        mixed = jnp.where(left, totals[m], totals[m + 1])
        send_ref[m // 2, TILES - 2] = mixed[:4]
        send_ref[m // 2, TILES - 1] = mixed[4:]
    for r in range(ROWS):
        mass_ref[r : r + 1, LANES:] = turn(base, -r)[0:1, :EXTRA]


def unpack_kernel(got_ref, winds_ref, fields_ref, extra_ref):
    extras = [
        jnp.concatenate([got_ref[owner, TILES - 2], got_ref[owner, TILES - 1]], axis=0)
        for owner in range(8)
    ]
    group = lax.broadcasted_iota(jnp.int32, (8, LANES), 1) // EXTRA
    for l in range(2):
        for r in range(ROWS):
            value = turn(extras[0], -4 * l - r)
            for owner in range(1, 8):
                value = jnp.where(group == owner, turn(extras[owner], owner - 4 * l - r), value)
            extra_ref[pl.ds(32 * l + r, 8, stride=4), :] = value
    group = group[:4]
    for f in range(8):
        if f == 2:
            continue
        for l in range(2):
            ref, at = (winds_ref, f) if f < 2 else (fields_ref, f - 3)
            extra = extra_ref[32 * l + 4 * f : 32 * l + 4 * f + 4, :]
            turned = [turn(got_ref[owner, tile_of(f, l)], owner) for owner in range(8)]
            for b in range(RADIX):
                if b == 0:
                    value = turned[0]
                else:
                    value = jnp.where(group == b - 1, extra, turned[b - 1])
                    if b < 8:
                        value = jnp.where(group < b, value, turned[b])
                ref[at, l, :, LANES * b : LANES * (b + 1)] = value


VMEM = pl.BlockSpec(memory_space=pltpu.VMEM)
HBM = pl.BlockSpec(memory_space=pltpu.HBM)
PARAMS = pltpu.CompilerParams(vmem_limit_bytes=24 * 1024 * 1024)


def shape(*sizes):
    return jax.ShapeDtypeStruct(sizes, jnp.float32)


def scratch(*sizes):
    return pltpu.VMEM(sizes, jnp.float32)


def shards(winds, fields, thickness, filter_mask, cutoff):
    table, high, low = (jnp.asarray(x) for x in make_tables())
    pairs = lax.axis_size("pair")
    mine, other = pl.pallas_call(
        pack_kernel,
        out_shape=[pltpu.VMEM((ROWS * RADIX + 1, 8, LANES), jnp.float32)] * 2,
        in_specs=[HBM] * 5,
        out_specs=[VMEM] * 2,
        scratch_shapes=[
            pltpu.SMEM((ROWS,), jnp.int32), pltpu.SMEM((ROWS,), jnp.int32),
            scratch(*winds.shape), scratch(*fields.shape), scratch(*thickness.shape),
            pltpu.SemaphoreType.DMA((5,)),
        ],
        compiler_params=pltpu.CompilerParams(vmem_limit_bytes=60 * 1024 * 1024),
    )(filter_mask, cutoff, winds, fields, thickness)
    bands = ("pair", "half")
    ups = [(2 * p + 1, 2 * p + 3) for p in range(pairs - 1)]
    downs = [(2 * p, 2 * p - 2) for p in range(1, pairs)]
    near = lax.ppermute(mine, bands, ups + downs)
    partner = lax.ppermute(other, bands, [(i, i ^ 1) for i in range(2 * pairs)])
    ups = [(2 * p, 2 * p + 2) for p in range(pairs - 1)]
    downs = [(2 * p + 1, 2 * p - 1) for p in range(1, pairs)]
    far = lax.ppermute(partner, bands, ups + downs)
    work = [
        scratch(16, LON), scratch(16, LANES), scratch(16, LANES), scratch(8, LON), scratch(16, LON),
        scratch(9, 8, LON),
    ]
    early, band = pl.pallas_call(
        early_kernel,
        out_shape=[
            pltpu.VMEM((2 * ROWS, 8, LON), jnp.float32), pltpu.VMEM((8, 9, 4, LANES), jnp.float32)
        ],
        in_specs=[VMEM] * 6,
        out_specs=[VMEM] * 2,
        scratch_shapes=[
            scratch(3 * ROWS, 8, LON), scratch(3, 8, LANES), scratch(ROWS, 8, LON),
            scratch(256, LANES),
        ] + work,
        compiler_params=PARAMS,
        cost_estimate=pl.CostEstimate(flops=0, bytes_accessed=3_000_000, transcendentals=0),
    )(mine, partner, near, table, high, low)
    send = pl.pallas_call(
        late_kernel,
        out_shape=shape(16, 9, 4, LANES),
        in_specs=[VMEM] * 7,
        out_specs=VMEM,
        scratch_shapes=[
            scratch(2 * ROWS, 8, LON), scratch(2, 8, LANES), scratch(ROWS, 8, LON),
            scratch(2 * ROWS, 8, LON), scratch(ROWS, 8, LON), scratch(256, LANES),
        ] + work,
        compiler_params=PARAMS,
    )(mine, far, early, band, table, high, low)
    got = lax.all_to_all(send, ("half", "lev"), split_axis=0, concat_axis=0, tiled=True)
    send, mass = pl.pallas_call(
        remap_kernel,
        out_shape=[pltpu.VMEM((8, TILES, 4, LANES), jnp.float32), shape(4, LANES + EXTRA)],
        in_specs=[VMEM],
        out_specs=[VMEM] * 2,
        scratch_shapes=[scratch(17, 8, LANES)],
        compiler_params=PARAMS,
    )(got)
    got = lax.all_to_all(send, "lev", split_axis=0, concat_axis=0, tiled=True)
    winds_out, fields_out = pl.pallas_call(
        unpack_kernel,
        out_shape=[shape(2, 2, 4, LON), shape(5, 2, 4, LON)],
        in_specs=[VMEM],
        out_specs=[VMEM] * 2,
        scratch_shapes=[scratch(64, LANES)],
        compiler_params=PARAMS,
    )(got)
    return winds_out, fields_out, mass


def solution(mesh):
    devices = mesh.devices
    mesh = jax.sharding.Mesh(
        devices.reshape(devices.shape[0] // 2, 2, devices.shape[1]), ("pair", "half", "lev")
    )
    lat = ("pair", "half")
    return jax.shard_map(
        shards,
        mesh=mesh,
        in_specs=(
            P(None, "lev", lat, None),
            P(None, "lev", lat, None),
            P("lev", lat, None),
            P(lat),
            P(lat),
        ),
        out_specs=(P(None, "lev", lat, None), P(None, "lev", lat, None), P(lat, "lev")),
        check_vma=False,
    )
```

```python
import math

import jax
import jax.numpy as jnp
import numpy as np
from jax import lax
from jax.experimental import pallas as pl
from jax.experimental.pallas import tpu as pltpu
from jax.sharding import PartitionSpec as P

NSUB = 2
COEF = 0.08
LANES = 128
RADIX = 9
LON = RADIX * LANES
HALF = RADIX // 2 + 1
ROWS = 4
TILES = 16
EXTRA = 16


def make_tables():
    n2 = np.arange(LANES)
    k1 = np.arange(HALF)
    theta = 2.0 * math.pi * k1[:, None] * n2[None, :] / LON
    k = k1[:, None] + RADIX * n2[None, :]
    k = np.minimum(k, LON - k)
    inverse = np.where(k > 0, 1.0 / np.maximum(k, 1) ** 2, 0.0)
    scale = np.where(k > 0, np.where(k1[:, None] == 0, 1.0, 2.0) / LON, 0.0)
    table = np.zeros((4, 8, LANES), np.float32)
    table[0, :HALF] = np.cos(theta)
    table[1, :HALF] = np.sin(theta)
    table[2, :HALF] = inverse
    table[3, :HALF] = scale
    angle = 2.0 * math.pi * (n2[:, None] * n2[None, :] % LANES) / LANES
    cosine, sine = np.cos(angle), np.sin(angle)
    dense = np.block([[cosine, -sine], [sine, cosine]]).astype(np.float32)
    high = dense.astype(jnp.bfloat16)
    low = (dense - high.astype(np.float32)).astype(jnp.bfloat16)
    return table, high, low


def split_dot(left, high, low):
    rows = left.shape[0]
    left_high = left.astype(jnp.bfloat16)
    coarse = left_high.astype(jnp.float32)
    stacked = jnp.concatenate([coarse, left - coarse], axis=0).astype(jnp.bfloat16)
    dot = lambda a, b: jnp.dot(a, b, preferred_element_type=jnp.float32)
    both = dot(stacked, high)
    return both[:rows] + (both[rows:] + dot(left_high, low))


def polar_filter(rows, wind_ref, square_ref, keep_ref, table_ref, high_ref, low_ref):
    blocks = [wind_ref[:rows, LANES * j : LANES * (j + 1)] for j in range(RADIX)]
    plus = [blocks[j] + blocks[RADIX - j] for j in range(1, HALF)]
    minus = [blocks[j] - blocks[RADIX - j] for j in range(1, HALF)]
    cosine = lambda a: math.cos(2.0 * math.pi * (a % RADIX) / RADIX)
    sine = lambda a: math.sin(2.0 * math.pi * (a % RADIX) / RADIX)
    real, imag = [blocks[0] + ((plus[0] + plus[1]) + (plus[2] + plus[3]))], [jnp.zeros_like(blocks[0])]
    for k in range(1, HALF):
        re = blocks[0]
        im = None
        for j in range(1, HALF):
            re = re + cosine(j * k) * plus[j - 1]
            term = sine(j * k) * minus[j - 1]
            im = -term if im is None else im - term
        turn_c = table_ref[0, k : k + 1, :]
        turn_s = table_ref[1, k : k + 1, :]
        real.append(re * turn_c + im * turn_s)
        imag.append(im * turn_c - re * turn_s)
    stacked = jnp.concatenate(
        [jnp.concatenate(real, axis=0), jnp.concatenate(imag, axis=0)], axis=1
    )
    high, low = high_ref[...], low_ref[...]
    spectra = split_dot(stacked, high, low)
    square, keep = square_ref[:rows], keep_ref[:rows]
    damped_re, damped_im = [], []
    for k in range(HALF):
        damp = jnp.maximum(0.0, 1.0 - square * table_ref[2, k : k + 1, :])
        damp = damp * (keep * table_ref[3, k : k + 1, :])
        damped_re.append(spectra[rows * k : rows * (k + 1), :LANES] * damp)
        damped_im.append(spectra[rows * k : rows * (k + 1), LANES:] * -damp)
    damped = jnp.concatenate(
        [jnp.concatenate(damped_re, axis=0), jnp.concatenate(damped_im, axis=0)], axis=1
    )
    back = split_dot(damped, high, low)
    first = back[:rows, :LANES]
    real, imag = [], []
    for k in range(1, HALF):
        re = back[rows * k : rows * (k + 1), :LANES]
        im = back[rows * k : rows * (k + 1), LANES:]
        turn_c = table_ref[0, k : k + 1, :]
        turn_s = table_ref[1, k : k + 1, :]
        real.append(re * turn_c + im * turn_s)
        imag.append(re * turn_s - im * turn_c)
    out = [blocks[0] - (first + ((real[0] + real[1]) + (real[2] + real[3])))] + [None] * (RADIX - 1)
    for n in range(1, HALF):
        even = first
        odd = None
        for k in range(1, HALF):
            even = even + cosine(n * k) * real[k - 1]
            term = sine(n * k) * imag[k - 1]
            odd = term if odd is None else odd + term
        out[n] = blocks[n] - (even - odd)
        out[RADIX - n] = blocks[RADIX - n] - (even + odd)
    return out


def face_weights(courant):
    up = jnp.maximum(courant, 0.0)
    down = jnp.minimum(courant, 0.0)
    a = 0.25 * up * (1.0 - up)
    d = 0.25 * down * (1.0 + down)
    return a, up + d, down + a, d


def advect_rows(count, row_of, store, u_ref, v_ref, weight_ref):
    for r in range(count):
        u_ref[r : r + 1, :] = row_of(r)[0:1]
    for r in range(-1, count + 1):
        v_ref[r + 1 : r + 2, :] = row_of(r)[1:2]
    u = COEF * u_ref[:count]
    a, b, c, d = face_weights(0.5 * (u + pltpu.roll(u, LON - 1, 1)))
    back = lambda x: pltpu.roll(x, 1, 1)
    weight_ref[0, :count] = -back(a)
    weight_ref[1, :count] = a + back(b)
    weight_ref[3, :count] = -(c + back(d))
    weight_ref[4, :count] = d
    center = 1.0 - (b - back(c))
    a, b, c, d = face_weights((0.5 * COEF) * (v_ref[: count + 1] + v_ref[1 : count + 2]))
    weight_ref[5, :count] = -a[:count]
    weight_ref[6, :count] = a[1:] + b[:count]
    weight_ref[2, :count] = center - (b[1:] - c[:count])
    weight_ref[7, :count] = -(c[1:] + d[:count])
    weight_ref[8, :count] = d[1:]
    for r in range(count):
        weight = lambda n: weight_ref[n, r : r + 1, :]
        q = row_of(r)
        new = weight(2) * q
        for n, step in ((0, 2), (1, 1), (3, LON - 1), (4, LON - 2)):
            new = new + weight(n) * pltpu.roll(q, step, 1)
        for n, step in ((5, -2), (6, -1), (7, 1), (8, 2)):
            new = new + weight(n) * row_of(r + step)
        store(r, new)


def pack_kernel(
    mask_hbm, cutoff_hbm, winds_hbm, fields_hbm, thick_hbm, mine_ref, other_ref,
    mask_ref, cutoff_ref, winds_ref, fields_ref, thick_ref, sems,
):
    copies = [
        pltpu.make_async_copy(source, target, sems.at[i])
        for i, (source, target) in enumerate(
            (
                (mask_hbm, mask_ref), (cutoff_hbm, cutoff_ref),
                (winds_hbm, winds_ref), (fields_hbm, fields_ref), (thick_hbm, thick_ref),
            )
        )
    ]
    for copy in copies:
        copy.start()
    half = lax.axis_index("half")
    copies[0].wait()
    copies[1].wait()
    for ref in (mine_ref, other_ref):
        for r in range(ROWS):
            cut = cutoff_ref[r].astype(jnp.float32)
            ref[ROWS * RADIX, r : r + 1, :] = jnp.full((1, LANES), cut * cut, jnp.float32)
            ref[ROWS * RADIX, ROWS + r : ROWS + r + 1, :] = jnp.full(
                (1, LANES), mask_ref[r].astype(jnp.float32), jnp.float32
            )
    for copy in copies[2:]:
        copy.wait()
    for ref, level in ((mine_ref, half), (other_ref, 1 - half)):
        for f in range(8):
            for r in range(ROWS):
                if f < 2:
                    row = winds_ref[f, level, r : r + 1, :]
                elif f == 2:
                    row = thick_ref[level, r : r + 1, :]
                else:
                    row = fields_ref[f - 3, level, r : r + 1, :]
                for b in range(RADIX):
                    ref[RADIX * r + b, f : f + 1, :] = row[:, LANES * b : LANES * (b + 1)]


def unpack_rows(parts, start_ref, meta_ref):
    for ref, group in parts:
        for r in range(ROWS):
            for b in range(RADIX):
                start_ref[ROWS * group + r, :, LANES * b : LANES * (b + 1)] = ref[RADIX * r + b]
        meta_ref[group] = ref[ROWS * RADIX]


def substep(count, row_of, meta_of, limit, target_ref, tables, work):
    wind_ref, square_ref, keep_ref, u_ref, v_ref, weight_ref = work

    def store(r, new):
        new = limit(r, new)
        target_ref[r] = new
        wind_ref[2 * r : 2 * r + 2, :] = new[0:2]

    advect_rows(count, row_of, store, u_ref, v_ref, weight_ref)
    for r in range(count):
        for ref, value in zip((square_ref, keep_ref), meta_of(r)):
            ref[2 * r : 2 * r + 2, :] = jnp.broadcast_to(value, (2, LANES))
    blocks = polar_filter(2 * count, wind_ref, square_ref, keep_ref, *tables)
    for j in range(RADIX):
        for r in range(count):
            target_ref[r, 0:2, LANES * j : LANES * (j + 1)] = blocks[j][2 * r : 2 * r + 2]


def meta_rows(meta_ref, first):
    def meta_of(r):
        group, at = (first + r) // ROWS, (first + r) % ROWS
        return meta_ref[group, at : at + 1, :], meta_ref[group, ROWS + at : ROWS + at + 1, :]

    return meta_of


def outside(r, count, edge):
    half = lax.axis_index("half")
    pair = lax.axis_index("pair")
    if r < 2:
        return jnp.logical_and(half == edge, pair == 0)
    if r >= count - 2:
        return jnp.logical_and(half == 1 - edge, pair == lax.axis_size("pair") - 1)
    return None


def limiter(count, edge):
    def limit(r, new):
        beyond = outside(r, count, edge)
        return new if beyond is None else jnp.where(beyond, 0.0, new)

    return limit


def pack_band(final_ref, put, turned_ref):
    group = lax.broadcasted_iota(jnp.int32, (8, LANES), 1) // EXTRA
    extras = [None] * 8
    for r in range(ROWS):
        blocks = [final_ref[r, :, LANES * b : LANES * (b + 1)] for b in range(RADIX)]
        for owner in range(8):
            value = jnp.where(
                group < 8 - owner, turn(blocks[owner], -owner), turn(blocks[owner + 1], -owner)
            )
            turned_ref[pl.ds(32 * owner + r, 8, stride=4), :] = value
            extra = turn(blocks[owner + 1], r - owner)
            extras[owner] = extra if r == 0 else jnp.where(group == r, extra, extras[owner])
    for owner in range(8):
        put(owner, 8, jnp.where(group[:4] < 4, extras[owner][:4], swap(extras[owner])[4:]))
        for f in range(8):
            put(owner, f, turned_ref[32 * owner + 4 * f : 32 * owner + 4 * f + 4, :])


def early_kernel(
    mine_ref, partner_ref, near_ref, table_ref, high_ref, low_ref, early_ref, band_ref,
    start_ref, meta_ref, final_ref, turned_ref, *work,
):
    half = lax.axis_index("half")
    tables = (table_ref, high_ref, low_ref)
    unpack_rows(
        ((mine_ref, 2 * half), (partner_ref, 1), (near_ref, 2 - 2 * half)), start_ref, meta_ref
    )
    substep(
        2 * ROWS, lambda r: start_ref[r + 2], meta_rows(meta_ref, 2), limiter(2 * ROWS, 1),
        early_ref, tables, work,
    )
    substep(
        ROWS, lambda r: early_ref[r + 2], meta_rows(meta_ref, ROWS), lambda r, new: new, final_ref,
        tables, work,
    )

    def put(owner, tile, value):
        band_ref[owner, tile] = value

    pack_band(final_ref, put, turned_ref)


def late_kernel(
    mine_ref, far_ref, early_ref, band_ref, table_ref, high_ref, low_ref, send_ref,
    start_ref, meta_ref, rest_ref, first_ref, final_ref, turned_ref, *work,
):
    half = lax.axis_index("half")
    tables = (table_ref, high_ref, low_ref)
    for owner in range(8):
        send_ref[8 * (1 - half) + owner] = band_ref[owner]
    for r in range(ROWS):
        first_ref[ROWS * (1 - half) + r] = early_ref[ROWS * half + r]
    unpack_rows(((mine_ref, 1 - half), (far_ref, half)), start_ref, meta_ref)
    substep(
        ROWS, lambda r: start_ref[r + 2], meta_rows(meta_ref, 2), limiter(ROWS, 0), rest_ref, tables,
        work,
    )
    for r in range(ROWS):
        first_ref[ROWS * half + r] = rest_ref[r]
    meta_ref[0] = mine_ref[ROWS * RADIX]
    substep(
        ROWS, lambda r: first_ref[r + 2], meta_rows(meta_ref, 0), lambda r, new: new, final_ref,
        tables, work,
    )

    def put(owner, tile, value):
        send_ref[8 * half + owner, tile] = value

    pack_band(final_ref, put, turned_ref)


def turn(x, steps):
    return pltpu.roll(x, EXTRA * (steps % 8), 1) if steps % 8 else x


def swap(x):
    return turn(x, 4)


def tile_of(f, level):
    return 7 * level + (f if f < 2 else f - 1)


def remap_kernel(got_ref, send_ref, mass_ref, edge_ref):
    levels = 16
    pairs = ((0, 1), (3, 4), (5, 6), (7, 7))
    both = lambda source, a, b: jnp.concatenate([got_ref[source, a], got_ref[source, b]], axis=0)
    inside = lambda lower, upper, low, high: jnp.maximum(
        0.0, jnp.minimum(upper, high) - jnp.maximum(lower, low)
    )
    add = lambda total, term: term if total is None else total + term

    edges = [jnp.zeros((8, LANES), jnp.float32)]
    for k in range(levels):
        edges.append(edges[-1] + both(8 * (k % 2) + k // 2, 2, 2))
    mass = edges[-1]
    scale = float(levels) / mass
    for i in range(levels + 1):
        edge_ref[i] = edges[i]
    chunk = 8
    for first in range(0, levels, chunk):
        bounds = [mass * (m / levels) for m in range(first, first + chunk + 1)]
        totals = [[None] * len(pairs) for _ in range(chunk)]
        for k in range(levels):
            lower, upper = edge_ref[k], edge_ref[k + 1]
            values = [both(8 * (k % 2) + k // 2, a, b) for a, b in pairs]
            for m in range(chunk):
                overlap = inside(lower, upper, bounds[m], bounds[m + 1])
                for p, value in enumerate(values):
                    totals[m][p] = add(totals[m][p], value * overlap)
        for m in range(chunk):
            target, level = (first + m) // 2, (first + m) % 2
            for p, (a, b) in enumerate(pairs):
                total = totals[m][p] * scale
                send_ref[target, tile_of(a, level)] = total[:4]
                if b != a:
                    send_ref[target, tile_of(b, level)] = total[4:]
    mass_ref[:, :LANES] = mass[:4]

    left = lax.broadcasted_iota(jnp.int32, (8, LANES), 1) < LANES // 2
    base = jnp.zeros((8, LANES), jnp.float32)
    steps = []
    for k in range(levels // 2):
        even, odd = got_ref[k, 8], got_ref[8 + k, 8]
        value = jnp.concatenate(
            [jnp.where(left[:4], even, swap(odd)), jnp.where(left[:4], swap(even), odd)], axis=0
        )
        thick = jnp.broadcast_to(value[2:3], (8, LANES))
        other = swap(thick)
        lower = base + jnp.where(left, 0.0, other)
        upper = lower + thick
        base = jnp.where(left, upper + other, upper)
        steps.append((value, lower, upper))
    scale = float(levels) / base
    bounds = [base * (m / levels) for m in range(levels + 1)]
    totals = [None] * levels
    for value, lower, upper in steps:
        for m in range(levels):
            totals[m] = add(totals[m], value * inside(lower, upper, bounds[m], bounds[m + 1]))
    totals = [(total + swap(total)) * scale for total in totals]
    for m in range(0, levels, 2):
        mixed = jnp.where(left, totals[m], totals[m + 1])
        send_ref[m // 2, TILES - 2] = mixed[:4]
        send_ref[m // 2, TILES - 1] = mixed[4:]
    for r in range(ROWS):
        mass_ref[r : r + 1, LANES:] = turn(base, -r)[0:1, :EXTRA]


def unpack_kernel(got_ref, winds_ref, fields_ref, extra_ref):
    extras = [
        jnp.concatenate([got_ref[owner, TILES - 2], got_ref[owner, TILES - 1]], axis=0)
        for owner in range(8)
    ]
    group = lax.broadcasted_iota(jnp.int32, (8, LANES), 1) // EXTRA
    for l in range(2):
        for r in range(ROWS):
            value = turn(extras[0], -4 * l - r)
            for owner in range(1, 8):
                value = jnp.where(group == owner, turn(extras[owner], owner - 4 * l - r), value)
            extra_ref[pl.ds(32 * l + r, 8, stride=4), :] = value
    group = group[:4]
    for f in range(8):
        if f == 2:
            continue
        for l in range(2):
            ref, at = (winds_ref, f) if f < 2 else (fields_ref, f - 3)
            extra = extra_ref[32 * l + 4 * f : 32 * l + 4 * f + 4, :]
            turned = [turn(got_ref[owner, tile_of(f, l)], owner) for owner in range(8)]
            for b in range(RADIX):
                if b == 0:
                    value = turned[0]
                else:
                    value = jnp.where(group == b - 1, extra, turned[b - 1])
                    if b < 8:
                        value = jnp.where(group < b, value, turned[b])
                ref[at, l, :, LANES * b : LANES * (b + 1)] = value


VMEM = pl.BlockSpec(memory_space=pltpu.VMEM)
HBM = pl.BlockSpec(memory_space=pltpu.HBM)
PARAMS = pltpu.CompilerParams(vmem_limit_bytes=24 * 1024 * 1024)


def shape(*sizes):
    return jax.ShapeDtypeStruct(sizes, jnp.float32)


def scratch(*sizes):
    return pltpu.VMEM(sizes, jnp.float32)


def shards(winds, fields, thickness, filter_mask, cutoff):
    table, high, low = (jnp.asarray(x) for x in make_tables())
    pairs = lax.axis_size("pair")
    mine, other = pl.pallas_call(
        pack_kernel,
        out_shape=[pltpu.VMEM((ROWS * RADIX + 1, 8, LANES), jnp.float32)] * 2,
        in_specs=[HBM] * 5,
        out_specs=[VMEM] * 2,
        scratch_shapes=[
            pltpu.SMEM((ROWS,), jnp.int32), pltpu.SMEM((ROWS,), jnp.int32),
            scratch(*winds.shape), scratch(*fields.shape), scratch(*thickness.shape),
            pltpu.SemaphoreType.DMA((5,)),
        ],
        compiler_params=pltpu.CompilerParams(vmem_limit_bytes=60 * 1024 * 1024),
    )(filter_mask, cutoff, winds, fields, thickness)
    bands = ("pair", "half")
    ups = [(2 * p + 1, 2 * p + 3) for p in range(pairs - 1)]
    downs = [(2 * p, 2 * p - 2) for p in range(1, pairs)]
    near = lax.ppermute(mine, bands, ups + downs)
    partner = lax.ppermute(other, bands, [(i, i ^ 1) for i in range(2 * pairs)])
    ups = [(2 * p, 2 * p + 2) for p in range(pairs - 1)]
    downs = [(2 * p + 1, 2 * p - 1) for p in range(1, pairs)]
    far = lax.ppermute(partner, bands, ups + downs)
    work = [
        scratch(16, LON), scratch(16, LANES), scratch(16, LANES), scratch(8, LON), scratch(16, LON),
        scratch(9, 8, LON),
    ]
    early, band = pl.pallas_call(
        early_kernel,
        out_shape=[
            pltpu.VMEM((2 * ROWS, 8, LON), jnp.float32), pltpu.VMEM((8, 9, 4, LANES), jnp.float32)
        ],
        in_specs=[VMEM] * 6,
        out_specs=[VMEM] * 2,
        scratch_shapes=[
            scratch(3 * ROWS, 8, LON), scratch(3, 8, LANES), scratch(ROWS, 8, LON),
            scratch(256, LANES),
        ] + work,
        compiler_params=PARAMS,
        cost_estimate=pl.CostEstimate(flops=0, bytes_accessed=3_000_000, transcendentals=0),
    )(mine, partner, near, table, high, low)
    send = pl.pallas_call(
        late_kernel,
        out_shape=shape(16, 9, 4, LANES),
        in_specs=[VMEM] * 7,
        out_specs=VMEM,
        scratch_shapes=[
            scratch(2 * ROWS, 8, LON), scratch(2, 8, LANES), scratch(ROWS, 8, LON),
            scratch(2 * ROWS, 8, LON), scratch(ROWS, 8, LON), scratch(256, LANES),
        ] + work,
        compiler_params=PARAMS,
    )(mine, far, early, band, table, high, low)
    got = lax.all_to_all(send, ("half", "lev"), split_axis=0, concat_axis=0, tiled=True)
    send, mass = pl.pallas_call(
        remap_kernel,
        out_shape=[pltpu.VMEM((8, TILES, 4, LANES), jnp.float32), shape(4, LANES + EXTRA)],
        in_specs=[VMEM],
        out_specs=[VMEM] * 2,
        scratch_shapes=[scratch(17, 8, LANES)],
        compiler_params=PARAMS,
    )(got)
    got = lax.all_to_all(send, "lev", split_axis=0, concat_axis=0, tiled=True)
    winds_out, fields_out = pl.pallas_call(
        unpack_kernel,
        out_shape=[shape(2, 2, 4, LON), shape(5, 2, 4, LON)],
        in_specs=[VMEM],
        out_specs=[VMEM] * 2,
        scratch_shapes=[scratch(64, LANES)],
        compiler_params=PARAMS,
    )(got)
    return winds_out, fields_out, mass


def solution(mesh):
    devices = mesh.devices
    mesh = jax.sharding.Mesh(
        devices.reshape(devices.shape[0] // 2, 2, devices.shape[1]), ("pair", "half", "lev")
    )
    lat = ("pair", "half")
    return jax.shard_map(
        shards,
        mesh=mesh,
        in_specs=(
            P(None, "lev", lat, None),
            P(None, "lev", lat, None),
            P("lev", lat, None),
            P(lat),
            P(lat),
        ),
        out_specs=(P(None, "lev", lat, None), P(None, "lev", lat, None), P(lat, "lev")),
        check_vma=False,
    )
```

```python
import math

import jax
import jax.numpy as jnp
import numpy as np
from jax import lax
from jax.experimental import pallas as pl
from jax.experimental.pallas import tpu as pltpu
from jax.sharding import PartitionSpec as P

NSUB = 2
COEF = 0.08
LANES = 128
RADIX = 9
LON = RADIX * LANES
HALF = RADIX // 2 + 1
ROWS = 4
TILES = 16
EXTRA = 16


def make_tables():
    n2 = np.arange(LANES)
    k1 = np.arange(HALF)
    theta = 2.0 * math.pi * k1[:, None] * n2[None, :] / LON
    k = k1[:, None] + RADIX * n2[None, :]
    k = np.minimum(k, LON - k)
    inverse = np.where(k > 0, 1.0 / np.maximum(k, 1) ** 2, 0.0)
    scale = np.where(k > 0, np.where(k1[:, None] == 0, 1.0, 2.0) / LON, 0.0)
    table = np.zeros((4, 8, LANES), np.float32)
    table[0, :HALF] = np.cos(theta)
    table[1, :HALF] = np.sin(theta)
    table[2, :HALF] = inverse
    table[3, :HALF] = scale
    angle = 2.0 * math.pi * (n2[:, None] * n2[None, :] % LANES) / LANES
    cosine, sine = np.cos(angle), np.sin(angle)
    dense = np.block([[cosine, -sine], [sine, cosine]]).astype(np.float32)
    high = dense.astype(jnp.bfloat16)
    low = (dense - high.astype(np.float32)).astype(jnp.bfloat16)
    return table, high, low


def split_dot(left, high, low):
    rows = left.shape[0]
    left_high = left.astype(jnp.bfloat16)
    coarse = left_high.astype(jnp.float32)
    stacked = jnp.concatenate([coarse, left - coarse], axis=0).astype(jnp.bfloat16)
    dot = lambda a, b: jnp.dot(a, b, preferred_element_type=jnp.float32)
    both = dot(stacked, high)
    return both[:rows] + (both[rows:] + dot(left_high, low))


def polar_filter(rows, wind_ref, square_ref, keep_ref, table_ref, high_ref, low_ref):
    blocks = [wind_ref[:rows, LANES * j : LANES * (j + 1)] for j in range(RADIX)]
    plus = [blocks[j] + blocks[RADIX - j] for j in range(1, HALF)]
    minus = [blocks[j] - blocks[RADIX - j] for j in range(1, HALF)]
    cosine = lambda a: math.cos(2.0 * math.pi * (a % RADIX) / RADIX)
    sine = lambda a: math.sin(2.0 * math.pi * (a % RADIX) / RADIX)
    real, imag = [blocks[0] + ((plus[0] + plus[1]) + (plus[2] + plus[3]))], [jnp.zeros_like(blocks[0])]
    for k in range(1, HALF):
        re = blocks[0]
        im = None
        for j in range(1, HALF):
            re = re + cosine(j * k) * plus[j - 1]
            term = sine(j * k) * minus[j - 1]
            im = -term if im is None else im - term
        turn_c = table_ref[0, k : k + 1, :]
        turn_s = table_ref[1, k : k + 1, :]
        real.append(re * turn_c + im * turn_s)
        imag.append(im * turn_c - re * turn_s)
    stacked = jnp.concatenate(
        [jnp.concatenate(real, axis=0), jnp.concatenate(imag, axis=0)], axis=1
    )
    high, low = high_ref[...], low_ref[...]
    spectra = split_dot(stacked, high, low)
    square, keep = square_ref[:rows], keep_ref[:rows]
    damped_re, damped_im = [], []
    for k in range(HALF):
        damp = jnp.maximum(0.0, 1.0 - square * table_ref[2, k : k + 1, :])
        damp = damp * (keep * table_ref[3, k : k + 1, :])
        damped_re.append(spectra[rows * k : rows * (k + 1), :LANES] * damp)
        damped_im.append(spectra[rows * k : rows * (k + 1), LANES:] * -damp)
    damped = jnp.concatenate(
        [jnp.concatenate(damped_re, axis=0), jnp.concatenate(damped_im, axis=0)], axis=1
    )
    back = split_dot(damped, high, low)
    first = back[:rows, :LANES]
    real, imag = [], []
    for k in range(1, HALF):
        re = back[rows * k : rows * (k + 1), :LANES]
        im = back[rows * k : rows * (k + 1), LANES:]
        turn_c = table_ref[0, k : k + 1, :]
        turn_s = table_ref[1, k : k + 1, :]
        real.append(re * turn_c + im * turn_s)
        imag.append(re * turn_s - im * turn_c)
    out = [blocks[0] - (first + ((real[0] + real[1]) + (real[2] + real[3])))] + [None] * (RADIX - 1)
    for n in range(1, HALF):
        even = first
        odd = None
        for k in range(1, HALF):
            even = even + cosine(n * k) * real[k - 1]
            term = sine(n * k) * imag[k - 1]
            odd = term if odd is None else odd + term
        out[n] = blocks[n] - (even - odd)
        out[RADIX - n] = blocks[RADIX - n] - (even + odd)
    return out


def face_weights(courant):
    up = jnp.maximum(courant, 0.0)
    down = jnp.minimum(courant, 0.0)
    a = 0.25 * up * (1.0 - up)
    d = 0.25 * down * (1.0 + down)
    return a, up + d, down + a, d


def advect_rows(count, row_of, store, u_ref, v_ref, weight_ref):
    for r in range(count):
        u_ref[r : r + 1, :] = row_of(r)[0:1]
    for r in range(-1, count + 1):
        v_ref[r + 1 : r + 2, :] = row_of(r)[1:2]
    u = COEF * u_ref[:count]
    a, b, c, d = face_weights(0.5 * (u + pltpu.roll(u, LON - 1, 1)))
    back = lambda x: pltpu.roll(x, 1, 1)
    weight_ref[0, :count] = -back(a)
    weight_ref[1, :count] = a + back(b)
    weight_ref[3, :count] = -(c + back(d))
    weight_ref[4, :count] = d
    center = 1.0 - (b - back(c))
    a, b, c, d = face_weights((0.5 * COEF) * (v_ref[: count + 1] + v_ref[1 : count + 2]))
    weight_ref[5, :count] = -a[:count]
    weight_ref[6, :count] = a[1:] + b[:count]
    weight_ref[2, :count] = center - (b[1:] - c[:count])
    weight_ref[7, :count] = -(c[1:] + d[:count])
    weight_ref[8, :count] = d[1:]
    for r in range(count):
        weight = lambda n: weight_ref[n, r : r + 1, :]
        q = row_of(r)
        new = weight(2) * q
        for n, step in ((0, 2), (1, 1), (3, LON - 1), (4, LON - 2)):
            new = new + weight(n) * pltpu.roll(q, step, 1)
        for n, step in ((5, -2), (6, -1), (7, 1), (8, 2)):
            new = new + weight(n) * row_of(r + step)
        store(r, new)


def pack_kernel(
    mask_hbm, cutoff_hbm, winds_hbm, fields_hbm, thick_hbm, mine_ref, other_ref,
    mask_ref, cutoff_ref, winds_ref, fields_ref, thick_ref, sems,
):
    copies = [
        pltpu.make_async_copy(source, target, sems.at[i])
        for i, (source, target) in enumerate(
            (
                (mask_hbm, mask_ref), (cutoff_hbm, cutoff_ref),
                (winds_hbm, winds_ref), (fields_hbm, fields_ref), (thick_hbm, thick_ref),
            )
        )
    ]
    for copy in copies:
        copy.start()
    half = lax.axis_index("half")
    copies[0].wait()
    copies[1].wait()
    for ref in (mine_ref, other_ref):
        for r in range(ROWS):
            cut = cutoff_ref[r].astype(jnp.float32)
            ref[ROWS * RADIX, r : r + 1, :] = jnp.full((1, LANES), cut * cut, jnp.float32)
            ref[ROWS * RADIX, ROWS + r : ROWS + r + 1, :] = jnp.full(
                (1, LANES), mask_ref[r].astype(jnp.float32), jnp.float32
            )
    for copy in copies[2:]:
        copy.wait()
    for ref, level in ((mine_ref, half), (other_ref, 1 - half)):
        for f in range(8):
            for r in range(ROWS):
                if f < 2:
                    row = winds_ref[f, level, r : r + 1, :]
                elif f == 2:
                    row = thick_ref[level, r : r + 1, :]
                else:
                    row = fields_ref[f - 3, level, r : r + 1, :]
                for b in range(RADIX):
                    ref[RADIX * r + b, f : f + 1, :] = row[:, LANES * b : LANES * (b + 1)]


def unpack_rows(parts, start_ref, meta_ref):
    for ref, group in parts:
        for r in range(ROWS):
            for b in range(RADIX):
                start_ref[ROWS * group + r, :, LANES * b : LANES * (b + 1)] = ref[RADIX * r + b]
        meta_ref[group] = ref[ROWS * RADIX]


def substep(count, row_of, meta_of, limit, target_ref, tables, work):
    wind_ref, square_ref, keep_ref, u_ref, v_ref, weight_ref = work

    def store(r, new):
        new = limit(r, new)
        target_ref[r] = new
        wind_ref[2 * r : 2 * r + 2, :] = new[0:2]

    advect_rows(count, row_of, store, u_ref, v_ref, weight_ref)
    for r in range(count):
        for ref, value in zip((square_ref, keep_ref), meta_of(r)):
            ref[2 * r : 2 * r + 2, :] = jnp.broadcast_to(value, (2, LANES))
    blocks = polar_filter(2 * count, wind_ref, square_ref, keep_ref, *tables)
    for j in range(RADIX):
        for r in range(count):
            target_ref[r, 0:2, LANES * j : LANES * (j + 1)] = blocks[j][2 * r : 2 * r + 2]


def meta_rows(meta_ref, first):
    def meta_of(r):
        group, at = (first + r) // ROWS, (first + r) % ROWS
        return meta_ref[group, at : at + 1, :], meta_ref[group, ROWS + at : ROWS + at + 1, :]

    return meta_of


def outside(r, count, edge):
    half = lax.axis_index("half")
    pair = lax.axis_index("pair")
    if r < 2:
        return jnp.logical_and(half == edge, pair == 0)
    if r >= count - 2:
        return jnp.logical_and(half == 1 - edge, pair == lax.axis_size("pair") - 1)
    return None


def limiter(count, edge):
    def limit(r, new):
        beyond = outside(r, count, edge)
        return new if beyond is None else jnp.where(beyond, 0.0, new)

    return limit


def pack_band(final_ref, put, turned_ref):
    group = lax.broadcasted_iota(jnp.int32, (8, LANES), 1) // EXTRA
    extras = [None] * 8
    for r in range(ROWS):
        blocks = [final_ref[r, :, LANES * b : LANES * (b + 1)] for b in range(RADIX)]
        for owner in range(8):
            value = jnp.where(
                group < 8 - owner, turn(blocks[owner], -owner), turn(blocks[owner + 1], -owner)
            )
            turned_ref[pl.ds(32 * owner + r, 8, stride=4), :] = value
            extra = turn(blocks[owner + 1], r - owner)
            extras[owner] = extra if r == 0 else jnp.where(group == r, extra, extras[owner])
    for owner in range(8):
        put(owner, 8, jnp.where(group[:4] < 4, extras[owner][:4], swap(extras[owner])[4:]))
        for f in range(8):
            put(owner, f, turned_ref[32 * owner + 4 * f : 32 * owner + 4 * f + 4, :])


def early_kernel(
    mine_ref, partner_ref, near_ref, table_ref, high_ref, low_ref, early_ref, band_ref,
    start_ref, meta_ref, final_ref, turned_ref, *work,
):
    half = lax.axis_index("half")
    tables = (table_ref, high_ref, low_ref)
    unpack_rows(
        ((mine_ref, 2 * half), (partner_ref, 1), (near_ref, 2 - 2 * half)), start_ref, meta_ref
    )
    substep(
        2 * ROWS, lambda r: start_ref[r + 2], meta_rows(meta_ref, 2), limiter(2 * ROWS, 1),
        early_ref, tables, work,
    )
    substep(
        ROWS, lambda r: early_ref[r + 2], meta_rows(meta_ref, ROWS), lambda r, new: new, final_ref,
        tables, work,
    )

    def put(owner, tile, value):
        band_ref[owner, tile] = value

    pack_band(final_ref, put, turned_ref)


def late_kernel(
    mine_ref, far_ref, early_ref, band_ref, table_ref, high_ref, low_ref, send_ref,
    start_ref, meta_ref, rest_ref, first_ref, final_ref, turned_ref, *work,
):
    half = lax.axis_index("half")
    tables = (table_ref, high_ref, low_ref)
    for owner in range(8):
        send_ref[2 * owner + 1 - half] = band_ref[owner]
    for r in range(ROWS):
        first_ref[ROWS * (1 - half) + r] = early_ref[ROWS * half + r]
    unpack_rows(((mine_ref, 1 - half), (far_ref, half)), start_ref, meta_ref)
    substep(
        ROWS, lambda r: start_ref[r + 2], meta_rows(meta_ref, 2), limiter(ROWS, 0), rest_ref, tables,
        work,
    )
    for r in range(ROWS):
        first_ref[ROWS * half + r] = rest_ref[r]
    meta_ref[0] = mine_ref[ROWS * RADIX]
    substep(
        ROWS, lambda r: first_ref[r + 2], meta_rows(meta_ref, 0), lambda r, new: new, final_ref,
        tables, work,
    )

    def put(owner, tile, value):
        send_ref[2 * owner + half, tile] = value

    pack_band(final_ref, put, turned_ref)


def turn(x, steps):
    return pltpu.roll(x, EXTRA * (steps % 8), 1) if steps % 8 else x


def swap(x):
    return turn(x, 4)


def tile_of(f, level):
    return 7 * level + (f if f < 2 else f - 1)


def remap_kernel(got_ref, send_ref, mass_ref, edge_ref):
    levels = 16
    pairs = ((0, 1), (3, 4), (5, 6), (7, 7))
    both = lambda source, a, b: jnp.concatenate([got_ref[source, a], got_ref[source, b]], axis=0)
    inside = lambda lower, upper, low, high: jnp.maximum(
        0.0, jnp.minimum(upper, high) - jnp.maximum(lower, low)
    )
    add = lambda total, term: term if total is None else total + term

    edges = [jnp.zeros((8, LANES), jnp.float32)]
    for k in range(levels):
        edges.append(edges[-1] + both(k, 2, 2))
    mass = edges[-1]
    scale = float(levels) / mass
    for i in range(levels + 1):
        edge_ref[i] = edges[i]
    chunk = 8
    for first in range(0, levels, chunk):
        bounds = [mass * (m / levels) for m in range(first, first + chunk + 1)]
        totals = [[None] * len(pairs) for _ in range(chunk)]
        for k in range(levels):
            lower, upper = edge_ref[k], edge_ref[k + 1]
            values = [both(k, a, b) for a, b in pairs]
            for m in range(chunk):
                overlap = inside(lower, upper, bounds[m], bounds[m + 1])
                for p, value in enumerate(values):
                    totals[m][p] = add(totals[m][p], value * overlap)
        for m in range(chunk):
            target, level = (first + m) // 2, (first + m) % 2
            for p, (a, b) in enumerate(pairs):
                total = totals[m][p] * scale
                send_ref[target, tile_of(a, level)] = total[:4]
                if b != a:
                    send_ref[target, tile_of(b, level)] = total[4:]
    mass_ref[:, :LANES] = mass[:4]

    left = lax.broadcasted_iota(jnp.int32, (8, LANES), 1) < LANES // 2
    base = jnp.zeros((8, LANES), jnp.float32)
    steps = []
    for k in range(levels // 2):
        even, odd = got_ref[2 * k, 8], got_ref[2 * k + 1, 8]
        value = jnp.concatenate(
            [jnp.where(left[:4], even, swap(odd)), jnp.where(left[:4], swap(even), odd)], axis=0
        )
        thick = jnp.broadcast_to(value[2:3], (8, LANES))
        other = swap(thick)
        lower = base + jnp.where(left, 0.0, other)
        upper = lower + thick
        base = jnp.where(left, upper + other, upper)
        steps.append((value, lower, upper))
    scale = float(levels) / base
    bounds = [base * (m / levels) for m in range(levels + 1)]
    totals = [None] * levels
    for value, lower, upper in steps:
        for m in range(levels):
            totals[m] = add(totals[m], value * inside(lower, upper, bounds[m], bounds[m + 1]))
    totals = [(total + swap(total)) * scale for total in totals]
    for m in range(0, levels, 2):
        mixed = jnp.where(left, totals[m], totals[m + 1])
        send_ref[m // 2, TILES - 2] = mixed[:4]
        send_ref[m // 2, TILES - 1] = mixed[4:]
    for r in range(ROWS):
        mass_ref[r : r + 1, LANES:] = turn(base, -r)[0:1, :EXTRA]


def unpack_kernel(got_ref, winds_ref, fields_ref, extra_ref):
    extras = [
        jnp.concatenate([got_ref[owner, TILES - 2], got_ref[owner, TILES - 1]], axis=0)
        for owner in range(8)
    ]
    group = lax.broadcasted_iota(jnp.int32, (8, LANES), 1) // EXTRA
    for l in range(2):
        for r in range(ROWS):
            value = turn(extras[0], -4 * l - r)
            for owner in range(1, 8):
                value = jnp.where(group == owner, turn(extras[owner], owner - 4 * l - r), value)
            extra_ref[pl.ds(32 * l + r, 8, stride=4), :] = value
    group = group[:4]
    for f in range(8):
        if f == 2:
            continue
        for l in range(2):
            ref, at = (winds_ref, f) if f < 2 else (fields_ref, f - 3)
            extra = extra_ref[32 * l + 4 * f : 32 * l + 4 * f + 4, :]
            turned = [turn(got_ref[owner, tile_of(f, l)], owner) for owner in range(8)]
            for b in range(RADIX):
                if b == 0:
                    value = turned[0]
                else:
                    value = jnp.where(group == b - 1, extra, turned[b - 1])
                    if b < 8:
                        value = jnp.where(group < b, value, turned[b])
                ref[at, l, :, LANES * b : LANES * (b + 1)] = value


VMEM = pl.BlockSpec(memory_space=pltpu.VMEM)
HBM = pl.BlockSpec(memory_space=pltpu.HBM)
PARAMS = pltpu.CompilerParams(vmem_limit_bytes=24 * 1024 * 1024)


def shape(*sizes):
    return jax.ShapeDtypeStruct(sizes, jnp.float32)


def scratch(*sizes):
    return pltpu.VMEM(sizes, jnp.float32)


def shards(winds, fields, thickness, filter_mask, cutoff):
    table, high, low = (jnp.asarray(x) for x in make_tables())
    pairs = lax.axis_size("pair")
    mine, other = pl.pallas_call(
        pack_kernel,
        out_shape=[pltpu.VMEM((ROWS * RADIX + 1, 8, LANES), jnp.float32)] * 2,
        in_specs=[HBM] * 5,
        out_specs=[VMEM] * 2,
        scratch_shapes=[
            pltpu.SMEM((ROWS,), jnp.int32), pltpu.SMEM((ROWS,), jnp.int32),
            scratch(*winds.shape), scratch(*fields.shape), scratch(*thickness.shape),
            pltpu.SemaphoreType.DMA((5,)),
        ],
        compiler_params=pltpu.CompilerParams(vmem_limit_bytes=60 * 1024 * 1024),
    )(filter_mask, cutoff, winds, fields, thickness)
    bands = ("pair", "half")
    ups = [(2 * p + 1, 2 * p + 3) for p in range(pairs - 1)]
    downs = [(2 * p, 2 * p - 2) for p in range(1, pairs)]
    near = lax.ppermute(mine, bands, ups + downs)
    partner = lax.ppermute(other, bands, [(i, i ^ 1) for i in range(2 * pairs)])
    ups = [(2 * p, 2 * p + 2) for p in range(pairs - 1)]
    downs = [(2 * p + 1, 2 * p - 1) for p in range(1, pairs)]
    far = lax.ppermute(partner, bands, ups + downs)
    work = [
        scratch(16, LON), scratch(16, LANES), scratch(16, LANES), scratch(8, LON), scratch(16, LON),
        scratch(9, 8, LON),
    ]
    early, band = pl.pallas_call(
        early_kernel,
        out_shape=[
            pltpu.VMEM((2 * ROWS, 8, LON), jnp.float32), pltpu.VMEM((8, 9, 4, LANES), jnp.float32)
        ],
        in_specs=[VMEM] * 6,
        out_specs=[VMEM] * 2,
        scratch_shapes=[
            scratch(3 * ROWS, 8, LON), scratch(3, 8, LANES), scratch(ROWS, 8, LON),
            scratch(256, LANES),
        ] + work,
        compiler_params=PARAMS,
        cost_estimate=pl.CostEstimate(flops=0, bytes_accessed=3_000_000, transcendentals=0),
    )(mine, partner, near, table, high, low)
    send = pl.pallas_call(
        late_kernel,
        out_shape=shape(16, 9, 4, LANES),
        in_specs=[VMEM] * 7,
        out_specs=VMEM,
        scratch_shapes=[
            scratch(2 * ROWS, 8, LON), scratch(2, 8, LANES), scratch(ROWS, 8, LON),
            scratch(2 * ROWS, 8, LON), scratch(ROWS, 8, LON), scratch(256, LANES),
        ] + work,
        compiler_params=PARAMS,
    )(mine, far, early, band, table, high, low)
    got = lax.all_to_all(send, ("lev", "half"), split_axis=0, concat_axis=0, tiled=True)
    send, mass = pl.pallas_call(
        remap_kernel,
        out_shape=[pltpu.VMEM((8, TILES, 4, LANES), jnp.float32), shape(4, LANES + EXTRA)],
        in_specs=[VMEM],
        out_specs=[VMEM] * 2,
        scratch_shapes=[scratch(17, 8, LANES)],
        compiler_params=PARAMS,
    )(got)
    got = lax.all_to_all(send, "lev", split_axis=0, concat_axis=0, tiled=True)
    winds_out, fields_out = pl.pallas_call(
        unpack_kernel,
        out_shape=[shape(2, 2, 4, LON), shape(5, 2, 4, LON)],
        in_specs=[VMEM],
        out_specs=[VMEM] * 2,
        scratch_shapes=[scratch(64, LANES)],
        compiler_params=PARAMS,
    )(got)
    return winds_out, fields_out, mass


def solution(mesh):
    devices = mesh.devices
    mesh = jax.sharding.Mesh(
        devices.reshape(devices.shape[0] // 2, 2, devices.shape[1]), ("pair", "half", "lev")
    )
    lat = ("pair", "half")
    return jax.shard_map(
        shards,
        mesh=mesh,
        in_specs=(
            P(None, "lev", lat, None),
            P(None, "lev", lat, None),
            P("lev", lat, None),
            P(lat),
            P(lat),
        ),
        out_specs=(P(None, "lev", lat, None), P(None, "lev", lat, None), P(lat, "lev")),
        check_vma=False,
    )
```

```python
import math

import jax
import jax.numpy as jnp
import numpy as np
from jax import lax
from jax.experimental import pallas as pl
from jax.experimental.pallas import tpu as pltpu
from jax.sharding import PartitionSpec as P

NSUB = 2
COEF = 0.08
LANES = 128
RADIX = 9
LON = RADIX * LANES
HALF = RADIX // 2 + 1
ROWS = 4
TILES = 16
EXTRA = 16


def make_tables():
    n2 = np.arange(LANES)
    k1 = np.arange(HALF)
    theta = 2.0 * math.pi * k1[:, None] * n2[None, :] / LON
    k = k1[:, None] + RADIX * n2[None, :]
    k = np.minimum(k, LON - k)
    inverse = np.where(k > 0, 1.0 / np.maximum(k, 1) ** 2, 0.0)
    scale = np.where(k > 0, np.where(k1[:, None] == 0, 1.0, 2.0) / LON, 0.0)
    table = np.zeros((4, 8, LANES), np.float32)
    table[0, :HALF] = np.cos(theta)
    table[1, :HALF] = np.sin(theta)
    table[2, :HALF] = inverse
    table[3, :HALF] = scale
    angle = 2.0 * math.pi * (n2[:, None] * n2[None, :] % LANES) / LANES
    cosine, sine = np.cos(angle), np.sin(angle)
    dense = np.block([[cosine, -sine], [sine, cosine]]).astype(np.float32)
    high = dense.astype(jnp.bfloat16)
    low = (dense - high.astype(np.float32)).astype(jnp.bfloat16)
    return table, high, low


def split_dot(left, high, low):
    rows = left.shape[0]
    left_high = left.astype(jnp.bfloat16)
    coarse = left_high.astype(jnp.float32)
    stacked = jnp.concatenate([coarse, left - coarse], axis=0).astype(jnp.bfloat16)
    dot = lambda a, b: jnp.dot(a, b, preferred_element_type=jnp.float32)
    both = dot(stacked, high)
    return both[:rows] + (both[rows:] + dot(left_high, low))


def polar_filter(rows, wind_ref, square_ref, keep_ref, table_ref, high_ref, low_ref):
    blocks = [wind_ref[:rows, LANES * j : LANES * (j + 1)] for j in range(RADIX)]
    plus = [blocks[j] + blocks[RADIX - j] for j in range(1, HALF)]
    minus = [blocks[j] - blocks[RADIX - j] for j in range(1, HALF)]
    cosine = lambda a: math.cos(2.0 * math.pi * (a % RADIX) / RADIX)
    sine = lambda a: math.sin(2.0 * math.pi * (a % RADIX) / RADIX)
    real, imag = [blocks[0] + ((plus[0] + plus[1]) + (plus[2] + plus[3]))], [jnp.zeros_like(blocks[0])]
    for k in range(1, HALF):
        re = blocks[0]
        im = None
        for j in range(1, HALF):
            re = re + cosine(j * k) * plus[j - 1]
            term = sine(j * k) * minus[j - 1]
            im = -term if im is None else im - term
        turn_c = table_ref[0, k : k + 1, :]
        turn_s = table_ref[1, k : k + 1, :]
        real.append(re * turn_c + im * turn_s)
        imag.append(im * turn_c - re * turn_s)
    stacked = jnp.concatenate(
        [jnp.concatenate(real, axis=0), jnp.concatenate(imag, axis=0)], axis=1
    )
    high, low = high_ref[...], low_ref[...]
    spectra = split_dot(stacked, high, low)
    square, keep = square_ref[:rows], keep_ref[:rows]
    damped_re, damped_im = [], []
    for k in range(HALF):
        damp = jnp.maximum(0.0, 1.0 - square * table_ref[2, k : k + 1, :])
        damp = damp * (keep * table_ref[3, k : k + 1, :])
        damped_re.append(spectra[rows * k : rows * (k + 1), :LANES] * damp)
        damped_im.append(spectra[rows * k : rows * (k + 1), LANES:] * -damp)
    damped = jnp.concatenate(
        [jnp.concatenate(damped_re, axis=0), jnp.concatenate(damped_im, axis=0)], axis=1
    )
    back = split_dot(damped, high, low)
    first = back[:rows, :LANES]
    real, imag = [], []
    for k in range(1, HALF):
        re = back[rows * k : rows * (k + 1), :LANES]
        im = back[rows * k : rows * (k + 1), LANES:]
        turn_c = table_ref[0, k : k + 1, :]
        turn_s = table_ref[1, k : k + 1, :]
        real.append(re * turn_c + im * turn_s)
        imag.append(re * turn_s - im * turn_c)
    out = [blocks[0] - (first + ((real[0] + real[1]) + (real[2] + real[3])))] + [None] * (RADIX - 1)
    for n in range(1, HALF):
        even = first
        odd = None
        for k in range(1, HALF):
            even = even + cosine(n * k) * real[k - 1]
            term = sine(n * k) * imag[k - 1]
            odd = term if odd is None else odd + term
        out[n] = blocks[n] - (even - odd)
        out[RADIX - n] = blocks[RADIX - n] - (even + odd)
    return out


def face_weights(courant):
    up = jnp.maximum(courant, 0.0)
    down = jnp.minimum(courant, 0.0)
    a = 0.25 * up * (1.0 - up)
    d = 0.25 * down * (1.0 + down)
    return a, up + d, down + a, d


def advect_rows(count, row_of, store, u_ref, v_ref, weight_ref):
    for r in range(count):
        u_ref[r : r + 1, :] = row_of(r)[0:1]
    for r in range(-1, count + 1):
        v_ref[r + 1 : r + 2, :] = row_of(r)[1:2]
    u = COEF * u_ref[:count]
    a, b, c, d = face_weights(0.5 * (u + pltpu.roll(u, LON - 1, 1)))
    back = lambda x: pltpu.roll(x, 1, 1)
    weight_ref[0, :count] = -back(a)
    weight_ref[1, :count] = a + back(b)
    weight_ref[3, :count] = -(c + back(d))
    weight_ref[4, :count] = d
    center = 1.0 - (b - back(c))
    a, b, c, d = face_weights((0.5 * COEF) * (v_ref[: count + 1] + v_ref[1 : count + 2]))
    weight_ref[5, :count] = -a[:count]
    weight_ref[6, :count] = a[1:] + b[:count]
    weight_ref[2, :count] = center - (b[1:] - c[:count])
    weight_ref[7, :count] = -(c[1:] + d[:count])
    weight_ref[8, :count] = d[1:]
    for r in range(count):
        weight = lambda n: weight_ref[n, r : r + 1, :]
        q = row_of(r)
        new = weight(2) * q
        for n, step in ((0, 2), (1, 1), (3, LON - 1), (4, LON - 2)):
            new = new + weight(n) * pltpu.roll(q, step, 1)
        for n, step in ((5, -2), (6, -1), (7, 1), (8, 2)):
            new = new + weight(n) * row_of(r + step)
        store(r, new)


def pack_kernel(
    mask_hbm, cutoff_hbm, winds_hbm, fields_hbm, thick_hbm, mine_ref, other_ref,
    mask_ref, cutoff_ref, winds_ref, fields_ref, thick_ref, sems,
):
    copies = [
        pltpu.make_async_copy(source, target, sems.at[i])
        for i, (source, target) in enumerate(
            (
                (mask_hbm, mask_ref), (cutoff_hbm, cutoff_ref),
                (winds_hbm, winds_ref), (fields_hbm, fields_ref), (thick_hbm, thick_ref),
            )
        )
    ]
    for copy in copies:
        copy.start()
    half = lax.axis_index("half")
    copies[0].wait()
    copies[1].wait()
    for ref in (mine_ref, other_ref):
        for r in range(ROWS):
            cut = cutoff_ref[r].astype(jnp.float32)
            ref[ROWS * RADIX, r : r + 1, :] = jnp.full((1, LANES), cut * cut, jnp.float32)
            ref[ROWS * RADIX, ROWS + r : ROWS + r + 1, :] = jnp.full(
                (1, LANES), mask_ref[r].astype(jnp.float32), jnp.float32
            )
    copies[2].wait()
    copies[4].wait()
    for f in range(8):
        if f == 3:
            copies[3].wait()
        for ref, level in ((mine_ref, half), (other_ref, 1 - half)):
            for r in range(ROWS):
                if f < 2:
                    row = winds_ref[f, level, r : r + 1, :]
                elif f == 2:
                    row = thick_ref[level, r : r + 1, :]
                else:
                    row = fields_ref[f - 3, level, r : r + 1, :]
                for b in range(RADIX):
                    ref[RADIX * r + b, f : f + 1, :] = row[:, LANES * b : LANES * (b + 1)]


def unpack_rows(parts, start_ref, meta_ref):
    for ref, group in parts:
        for r in range(ROWS):
            for b in range(RADIX):
                start_ref[ROWS * group + r, :, LANES * b : LANES * (b + 1)] = ref[RADIX * r + b]
        meta_ref[group] = ref[ROWS * RADIX]


def substep(count, row_of, meta_of, limit, target_ref, tables, work):
    wind_ref, square_ref, keep_ref, u_ref, v_ref, weight_ref = work

    def store(r, new):
        new = limit(r, new)
        target_ref[r] = new
        wind_ref[2 * r : 2 * r + 2, :] = new[0:2]

    advect_rows(count, row_of, store, u_ref, v_ref, weight_ref)
    for r in range(count):
        for ref, value in zip((square_ref, keep_ref), meta_of(r)):
            ref[2 * r : 2 * r + 2, :] = jnp.broadcast_to(value, (2, LANES))
    blocks = polar_filter(2 * count, wind_ref, square_ref, keep_ref, *tables)
    for j in range(RADIX):
        for r in range(count):
            target_ref[r, 0:2, LANES * j : LANES * (j + 1)] = blocks[j][2 * r : 2 * r + 2]


def meta_rows(meta_ref, first):
    def meta_of(r):
        group, at = (first + r) // ROWS, (first + r) % ROWS
        return meta_ref[group, at : at + 1, :], meta_ref[group, ROWS + at : ROWS + at + 1, :]

    return meta_of


def outside(r, count, edge):
    half = lax.axis_index("half")
    pair = lax.axis_index("pair")
    if r < 2:
        return jnp.logical_and(half == edge, pair == 0)
    if r >= count - 2:
        return jnp.logical_and(half == 1 - edge, pair == lax.axis_size("pair") - 1)
    return None


def limiter(count, edge):
    def limit(r, new):
        beyond = outside(r, count, edge)
        return new if beyond is None else jnp.where(beyond, 0.0, new)

    return limit


def pack_band(final_ref, put, turned_ref):
    group = lax.broadcasted_iota(jnp.int32, (8, LANES), 1) // EXTRA
    extras = [None] * 8
    for r in range(ROWS):
        blocks = [final_ref[r, :, LANES * b : LANES * (b + 1)] for b in range(RADIX)]
        for owner in range(8):
            value = jnp.where(
                group < 8 - owner, turn(blocks[owner], -owner), turn(blocks[owner + 1], -owner)
            )
            turned_ref[pl.ds(32 * owner + r, 8, stride=4), :] = value
            extra = turn(blocks[owner + 1], r - owner)
            extras[owner] = extra if r == 0 else jnp.where(group == r, extra, extras[owner])
    for owner in range(8):
        put(owner, 8, jnp.where(group[:4] < 4, extras[owner][:4], swap(extras[owner])[4:]))
        for f in range(8):
            put(owner, f, turned_ref[32 * owner + 4 * f : 32 * owner + 4 * f + 4, :])


def early_kernel(
    mine_ref, partner_ref, near_ref, table_ref, high_ref, low_ref, early_ref, band_ref,
    start_ref, meta_ref, final_ref, turned_ref, *work,
):
    half = lax.axis_index("half")
    tables = (table_ref, high_ref, low_ref)
    unpack_rows(
        ((mine_ref, 2 * half), (partner_ref, 1), (near_ref, 2 - 2 * half)), start_ref, meta_ref
    )
    substep(
        2 * ROWS, lambda r: start_ref[r + 2], meta_rows(meta_ref, 2), limiter(2 * ROWS, 1),
        early_ref, tables, work,
    )
    substep(
        ROWS, lambda r: early_ref[r + 2], meta_rows(meta_ref, ROWS), lambda r, new: new, final_ref,
        tables, work,
    )

    def put(owner, tile, value):
        band_ref[owner, tile] = value

    pack_band(final_ref, put, turned_ref)


def late_kernel(
    mine_ref, far_ref, early_ref, band_ref, table_ref, high_ref, low_ref, send_ref,
    start_ref, meta_ref, rest_ref, first_ref, final_ref, turned_ref, *work,
):
    half = lax.axis_index("half")
    tables = (table_ref, high_ref, low_ref)
    for owner in range(8):
        send_ref[8 * (1 - half) + owner] = band_ref[owner]
    for r in range(ROWS):
        first_ref[ROWS * (1 - half) + r] = early_ref[ROWS * half + r]
    unpack_rows(((mine_ref, 1 - half), (far_ref, half)), start_ref, meta_ref)
    substep(
        ROWS, lambda r: start_ref[r + 2], meta_rows(meta_ref, 2), limiter(ROWS, 0), rest_ref, tables,
        work,
    )
    for r in range(ROWS):
        first_ref[ROWS * half + r] = rest_ref[r]
    meta_ref[0] = mine_ref[ROWS * RADIX]
    substep(
        ROWS, lambda r: first_ref[r + 2], meta_rows(meta_ref, 0), lambda r, new: new, final_ref,
        tables, work,
    )

    def put(owner, tile, value):
        send_ref[8 * half + owner, tile] = value

    pack_band(final_ref, put, turned_ref)


def turn(x, steps):
    return pltpu.roll(x, EXTRA * (steps % 8), 1) if steps % 8 else x


def swap(x):
    return turn(x, 4)


def tile_of(f, level):
    return 7 * level + (f if f < 2 else f - 1)


def remap_kernel(got_ref, send_ref, mass_ref, edge_ref):
    levels = 16
    pairs = ((0, 1), (3, 4), (5, 6), (7, 7))
    both = lambda source, a, b: jnp.concatenate([got_ref[source, a], got_ref[source, b]], axis=0)
    inside = lambda lower, upper, low, high: jnp.maximum(
        0.0, jnp.minimum(upper, high) - jnp.maximum(lower, low)
    )
    add = lambda total, term: term if total is None else total + term

    edges = [jnp.zeros((8, LANES), jnp.float32)]
    for k in range(levels):
        edges.append(edges[-1] + both(8 * (k % 2) + k // 2, 2, 2))
    mass = edges[-1]
    scale = float(levels) / mass
    for i in range(levels + 1):
        edge_ref[i] = edges[i]
    chunk = 8
    for first in range(0, levels, chunk):
        bounds = [mass * (m / levels) for m in range(first, first + chunk + 1)]
        totals = [[None] * len(pairs) for _ in range(chunk)]
        for k in range(levels):
            lower, upper = edge_ref[k], edge_ref[k + 1]
            values = [both(8 * (k % 2) + k // 2, a, b) for a, b in pairs]
            for m in range(chunk):
                overlap = inside(lower, upper, bounds[m], bounds[m + 1])
                for p, value in enumerate(values):
                    totals[m][p] = add(totals[m][p], value * overlap)
        for m in range(chunk):
            target, level = (first + m) // 2, (first + m) % 2
            for p, (a, b) in enumerate(pairs):
                total = totals[m][p] * scale
                send_ref[target, tile_of(a, level)] = total[:4]
                if b != a:
                    send_ref[target, tile_of(b, level)] = total[4:]
    mass_ref[:, :LANES] = mass[:4]

    left = lax.broadcasted_iota(jnp.int32, (8, LANES), 1) < LANES // 2
    base = jnp.zeros((8, LANES), jnp.float32)
    steps = []
    for k in range(levels // 2):
        even, odd = got_ref[k, 8], got_ref[8 + k, 8]
        value = jnp.concatenate(
            [jnp.where(left[:4], even, swap(odd)), jnp.where(left[:4], swap(even), odd)], axis=0
        )
        thick = jnp.broadcast_to(value[2:3], (8, LANES))
        other = swap(thick)
        lower = base + jnp.where(left, 0.0, other)
        upper = lower + thick
        base = jnp.where(left, upper + other, upper)
        steps.append((value, lower, upper))
    scale = float(levels) / base
    bounds = [base * (m / levels) for m in range(levels + 1)]
    totals = [None] * levels
    for value, lower, upper in steps:
        for m in range(levels):
            totals[m] = add(totals[m], value * inside(lower, upper, bounds[m], bounds[m + 1]))
    totals = [(total + swap(total)) * scale for total in totals]
    for m in range(0, levels, 2):
        mixed = jnp.where(left, totals[m], totals[m + 1])
        send_ref[m // 2, TILES - 2] = mixed[:4]
        send_ref[m // 2, TILES - 1] = mixed[4:]
    for r in range(ROWS):
        mass_ref[r : r + 1, LANES:] = turn(base, -r)[0:1, :EXTRA]


def unpack_kernel(got_ref, winds_ref, fields_ref, extra_ref):
    extras = [
        jnp.concatenate([got_ref[owner, TILES - 2], got_ref[owner, TILES - 1]], axis=0)
        for owner in range(8)
    ]
    group = lax.broadcasted_iota(jnp.int32, (8, LANES), 1) // EXTRA
    for l in range(2):
        for r in range(ROWS):
            value = turn(extras[0], -4 * l - r)
            for owner in range(1, 8):
                value = jnp.where(group == owner, turn(extras[owner], owner - 4 * l - r), value)
            extra_ref[pl.ds(32 * l + r, 8, stride=4), :] = value
    group = group[:4]
    for f in range(8):
        if f == 2:
            continue
        for l in range(2):
            ref, at = (winds_ref, f) if f < 2 else (fields_ref, f - 3)
            extra = extra_ref[32 * l + 4 * f : 32 * l + 4 * f + 4, :]
            turned = [turn(got_ref[owner, tile_of(f, l)], owner) for owner in range(8)]
            for b in range(RADIX):
                if b == 0:
                    value = turned[0]
                else:
                    value = jnp.where(group == b - 1, extra, turned[b - 1])
                    if b < 8:
                        value = jnp.where(group < b, value, turned[b])
                ref[at, l, :, LANES * b : LANES * (b + 1)] = value


VMEM = pl.BlockSpec(memory_space=pltpu.VMEM)
HBM = pl.BlockSpec(memory_space=pltpu.HBM)
PARAMS = pltpu.CompilerParams(vmem_limit_bytes=24 * 1024 * 1024)


def shape(*sizes):
    return jax.ShapeDtypeStruct(sizes, jnp.float32)


def scratch(*sizes):
    return pltpu.VMEM(sizes, jnp.float32)


def shards(winds, fields, thickness, filter_mask, cutoff):
    table, high, low = (jnp.asarray(x) for x in make_tables())
    pairs = lax.axis_size("pair")
    mine, other = pl.pallas_call(
        pack_kernel,
        out_shape=[pltpu.VMEM((ROWS * RADIX + 1, 8, LANES), jnp.float32)] * 2,
        in_specs=[HBM] * 5,
        out_specs=[VMEM] * 2,
        scratch_shapes=[
            pltpu.SMEM((ROWS,), jnp.int32), pltpu.SMEM((ROWS,), jnp.int32),
            scratch(*winds.shape), scratch(*fields.shape), scratch(*thickness.shape),
            pltpu.SemaphoreType.DMA((5,)),
        ],
        compiler_params=pltpu.CompilerParams(vmem_limit_bytes=60 * 1024 * 1024),
    )(filter_mask, cutoff, winds, fields, thickness)
    bands = ("pair", "half")
    ups = [(2 * p + 1, 2 * p + 3) for p in range(pairs - 1)]
    downs = [(2 * p, 2 * p - 2) for p in range(1, pairs)]
    near = lax.ppermute(mine, bands, ups + downs)
    partner = lax.ppermute(other, bands, [(i, i ^ 1) for i in range(2 * pairs)])
    ups = [(2 * p, 2 * p + 2) for p in range(pairs - 1)]
    downs = [(2 * p + 1, 2 * p - 1) for p in range(1, pairs)]
    far = lax.ppermute(partner, bands, ups + downs)
    work = [
        scratch(16, LON), scratch(16, LANES), scratch(16, LANES), scratch(8, LON), scratch(16, LON),
        scratch(9, 8, LON),
    ]
    early, band = pl.pallas_call(
        early_kernel,
        out_shape=[
            pltpu.VMEM((2 * ROWS, 8, LON), jnp.float32), pltpu.VMEM((8, 9, 4, LANES), jnp.float32)
        ],
        in_specs=[VMEM] * 6,
        out_specs=[VMEM] * 2,
        scratch_shapes=[
            scratch(3 * ROWS, 8, LON), scratch(3, 8, LANES), scratch(ROWS, 8, LON),
            scratch(256, LANES),
        ] + work,
        compiler_params=PARAMS,
        cost_estimate=pl.CostEstimate(flops=0, bytes_accessed=3_000_000, transcendentals=0),
    )(mine, partner, near, table, high, low)
    send = pl.pallas_call(
        late_kernel,
        out_shape=shape(16, 9, 4, LANES),
        in_specs=[VMEM] * 7,
        out_specs=VMEM,
        scratch_shapes=[
            scratch(2 * ROWS, 8, LON), scratch(2, 8, LANES), scratch(ROWS, 8, LON),
            scratch(2 * ROWS, 8, LON), scratch(ROWS, 8, LON), scratch(256, LANES),
        ] + work,
        compiler_params=PARAMS,
    )(mine, far, early, band, table, high, low)
    got = lax.all_to_all(send, ("half", "lev"), split_axis=0, concat_axis=0, tiled=True)
    send, mass = pl.pallas_call(
        remap_kernel,
        out_shape=[pltpu.VMEM((8, TILES, 4, LANES), jnp.float32), shape(4, LANES + EXTRA)],
        in_specs=[VMEM],
        out_specs=[VMEM] * 2,
        scratch_shapes=[scratch(17, 8, LANES)],
        compiler_params=PARAMS,
    )(got)
    got = lax.all_to_all(send, "lev", split_axis=0, concat_axis=0, tiled=True)
    winds_out, fields_out = pl.pallas_call(
        unpack_kernel,
        out_shape=[shape(2, 2, 4, LON), shape(5, 2, 4, LON)],
        in_specs=[VMEM],
        out_specs=[VMEM] * 2,
        scratch_shapes=[scratch(64, LANES)],
        compiler_params=PARAMS,
    )(got)
    return winds_out, fields_out, mass


def solution(mesh):
    devices = mesh.devices
    mesh = jax.sharding.Mesh(
        devices.reshape(devices.shape[0] // 2, 2, devices.shape[1]), ("pair", "half", "lev")
    )
    lat = ("pair", "half")
    return jax.shard_map(
        shards,
        mesh=mesh,
        in_specs=(
            P(None, "lev", lat, None),
            P(None, "lev", lat, None),
            P("lev", lat, None),
            P(lat),
            P(lat),
        ),
        out_specs=(P(None, "lev", lat, None), P(None, "lev", lat, None), P(lat, "lev")),
        check_vma=False,
    )
```
